32 devices in a mesh: frag: 2 (over x), occ: 4 (over y, core), vir: 4 (over z).
Axes of the slice: x: 2, y: 2, z: 4, core: 2. Of those that a mesh axis runs over, the one named last changes fastest.
Arguments:
- amplitudes: bfloat16 [256, 4096], P(('frag', 'occ')), parts along dimension 0, may hold values from -6 to 6
- panels: bfloat16 [32, 64, 20480], P(('frag', 'occ'), None, 'vir'), parts along dimension 0, may hold values from -0.25 to 0.25
- tile_mask: int32 [32, 320], P(('frag', 'occ'), 'vir'), parts along dimension 0, may hold values 0 or 1
- ranks: int32 [32], P(('frag', 'occ')), parts along dimension 0, may hold values from 16 to 64
- tile_owner: int32 [256], P(('frag', 'occ')), parts along dimension 0, may hold values from 0 to 3, as said below
- tile_row: int32 [256], P(('frag', 'occ')), parts along dimension 0, may hold values from 0 to 3, as said below
- tile_block: int32 [256], P(('frag', 'occ')), parts along dimension 0, may hold values from 0 to 15, as said below
Outputs:
- residual: bfloat16 [32, 64, 20480], P(('frag', 'occ'), None, 'vir'), parts along dimension 0
The draws below stay inside these ranges and needn't reach their ends.
There are 2 independent parts, one for each index of `frag`. The reference program is written for one: setup_inputs(seed, part) draws one part's arguments, and reference() takes and returns one part's arrays. A program takes and returns all parts, laid end to end along the dimension named above; each array names one. Nothing has to cross between parts.
Inputs may be any that keep to these rules, and one draw needn't show every extreme that they name: `tile_owner`: among the 32 tiles of one occ index, one owner drawn per draw is named exactly 8 times by every index, and the other owners share the rest as evenly as possible (counts differ by at most one). No two tiles with the same owner share both tile_row and tile_block. `tile_block`: see tile_row.
All inputs are finite; a program needn't handle non-finite values. No bound on the sum of `tile_mask` on one device may be relied on, other than what follows from the above.
Results may differ from the reference program's by a relative error of at most 0.001.
Values may be sent and summed in bfloat16 or wider, within the bound.
A program may use at most 128 MiB of HBM per device.

```python
import jax
import jax.numpy as jnp
from jax import lax

TW = 64
NCOL = 20480
TILE_DEV = 32
ROW_DEV = 4
CAP = 8
TILES = 128
ROWS = 16
BLOCKS = 16
VT = 320
N_OCC = 4


def route_tables(key):
    key_busy, key_offsets, key_shuffle, key_cells = jax.random.split(key, 4)
    busiest = jax.random.randint(key_busy, (), 0, N_OCC)
    position = jnp.arange(TILE_DEV)
    source = jnp.arange(N_OCC)
    offsets = jax.random.randint(key_offsets, (N_OCC, 1), 0, N_OCC - 1)
    others = (position[None, :] - CAP + offsets) % (N_OCC - 1)
    others = others + (others >= busiest).astype(jnp.int32)
    sorted_owner = jnp.where(position[None, :] < CAP, busiest, others)
    shuffle = jax.vmap(lambda subkey: jax.random.permutation(subkey, TILE_DEV))(jax.random.split(key_shuffle, N_OCC))
    owner = jnp.take_along_axis(sorted_owner, shuffle, axis=1)
    onehot = (owner[:, :, None] == source[None, None, :]).astype(jnp.int32)
    before = jnp.sum((jnp.cumsum(onehot, axis=1) - onehot) * onehot, axis=2)
    arrival = source[:, None] * CAP + before
    cell_table = jax.vmap(lambda subkey: jax.random.permutation(subkey, ROW_DEV * BLOCKS))(jax.random.split(key_cells, N_OCC))
    cell_index = cell_table[owner, arrival]
    return (owner.reshape(TILES).astype(jnp.int32), (cell_index // BLOCKS).reshape(TILES).astype(jnp.int32), (cell_index % BLOCKS).reshape(TILES).astype(jnp.int32))


def draw_tile_owner(key, part):
    return route_tables(key)[0]


def draw_tile_row(key, part):
    return route_tables(key)[1]


def draw_tile_block(key, part):
    return route_tables(key)[2]


def set_ends(drawn, stream_key, least, high):
    longest = drawn.shape.index(max(drawn.shape))
    spots = []
    for shift in (0, 1):
        where = [jax.random.randint(jax.random.fold_in(stream_key, axis), (), 0, length) for axis, length in enumerate(drawn.shape)]
        where[longest] = (where[longest] + shift) % drawn.shape[longest]
        spots.append(tuple(where))
    return drawn.at[spots[0]].set(least).at[spots[1]].set(high)


def levels(own_key, extent, shards, low, top_value):
    def one(axis_at, shards_of):
        steps = jax.random.uniform(jax.random.fold_in(jax.random.fold_in(own_key, 6), axis_at), (shards_of,), jnp.float32, low / len(shards), top_value / len(shards))
        return jnp.repeat(jnp.exp(steps), extent[axis_at] // shards_of).reshape((-1,) + (1,) * (len(extent) - axis_at - 1))

    loudness = one(*shards[0])
    for cut in shards[1:]:
        loudness = loudness * one(*cut)
    return loudness


def gaussian(rng, extent, scale, limit, pieces=(), held_as=jnp.bfloat16):
    values = jax.random.normal(rng, extent, jnp.float32) * scale
    if len(pieces) > 0:
        values = levels(rng, extent, pieces, -0.22, 0.18) * values
    return jnp.clip(values, min=-limit, max=limit).astype(held_as)


def setup_inputs(seed: int = 0, part: int = 0) -> dict:
    keys = jax.random.split(jax.random.key(seed), 8)
    part_keys = jax.random.split(jax.random.fold_in(keys[7], part), 8)
    amplitudes = gaussian(part_keys[0], (TILES, TW * TW), 1.0, 6.0, ((0, 4),))
    panels = gaussian(part_keys[1], (BLOCKS, TW, NCOL), (TW * 8) ** -0.5, 0.25, ((0, 4), (2, 4)))
    tile_mask = set_ends((jax.random.randint(part_keys[2], (BLOCKS, VT), 0, 4) < 3).astype(jnp.int32), jax.random.fold_in(part_keys[2], 1), 0, 1)
    ranks = set_ends(jax.random.randint(part_keys[3], (ROWS,), 16, 65), jax.random.fold_in(part_keys[3], 1), 16, 64).astype(jnp.int32)
    tile_owner = draw_tile_owner(jax.random.fold_in(jax.random.fold_in(keys[7], part), 71), part)
    tile_row = draw_tile_row(jax.random.fold_in(jax.random.fold_in(keys[7], part), 71), part)
    tile_block = draw_tile_block(jax.random.fold_in(jax.random.fold_in(keys[7], part), 71), part)
    return dict(amplitudes=amplitudes, panels=panels, tile_mask=tile_mask, ranks=ranks, tile_owner=tile_owner, tile_row=tile_row, tile_block=tile_block)


def reference(amplitudes, panels, tile_mask, ranks, tile_owner, tile_row, tile_block):
    col_mask = jnp.repeat(tile_mask, TW, axis=1).astype(panels.dtype)
    masked = panels * col_mask[:, None, :]
    pair_rows = (tile_owner * ROW_DEV + tile_row).astype(jnp.int32)
    tile_rank = ranks[pair_rows]
    kept_mask = jnp.arange(TW)[None, :] < tile_rank[:, None]
    amp_tiles = amplitudes.reshape(TILES, TW, TW)
    amp_tiles = jnp.where(kept_mask[:, :, None] & kept_mask[:, None, :], amp_tiles, jnp.zeros_like(amp_tiles))

    def add_tile(running, element):
        one_tile, pair_row, block_id = element
        product = jnp.dot(one_tile, masked[block_id], preferred_element_type=jnp.float32)
        return running.at[pair_row].add(product), None

    running = jnp.zeros((ROWS, TW, NCOL), jnp.float32)
    running, unused = lax.scan(add_tile, running, (amp_tiles, pair_rows, tile_block.astype(jnp.int32)))
    return running.astype(jnp.bfloat16)
```

```python
import functools

import jax
import jax.numpy as jnp
from jax import lax
from jax.experimental import pallas as pl
from jax.experimental.pallas import tpu as pltpu
from jax.sharding import PartitionSpec as P

MESH = pl.DeviceIdType.MESH
CHUNK = 512
EARLY = 2


def kernel(
    n, row_dev, width, capacity,
    panel_hbm, amp_hbm, mask_ref, rank_ref, owner_ref, row_ref, block_ref,
    out_hbm,
    gathered, amp, outbox, inbox, code_out, code_in, cells_s, block_f32, block_bf, staged,
    load_sem, amp_sem, far_send, far_recv, mate_send, mate_recv, fwd_send, fwd_recv,
    box_send, box_recv, code_send, code_recv, out_sem,
):
    me = lax.axis_index("occ")
    ranks_of_chips = n // 2
    mate = me + 1 - 2 * lax.rem(me, 2)
    chunks = gathered.shape[0]
    depth = panel_hbm.shape[0]
    local_blocks = depth // width
    blocks = local_blocks * n
    tiles = amp.shape[0]
    flat = amp.shape[1]
    half = flat // 2
    cells = row_dev * blocks

    def peer(distance):
        return lax.rem(me + distance, n)

    def slot(k, source):
        return gathered.at[k, pl.ds(pl.multiple_of(source * depth, depth), depth), :]

    def columns(k):
        return pl.ds(pl.multiple_of(k * CHUNK, CHUNK), CHUNK)

    def load(k):
        return pltpu.make_async_copy(panel_hbm.at[:, columns(k)], slot(k, me), load_sem.at[k])

    def far(k, d):
        return pltpu.make_async_remote_copy(
            src_ref=slot(k, me), dst_ref=slot(k, me),
            send_sem=far_send.at[d - 1, k], recv_sem=far_recv.at[d - 1, k],
            device_id={"occ": peer(2 * d)}, device_id_type=MESH,
        )

    def near(k):
        return pltpu.make_async_remote_copy(
            src_ref=slot(k, me), dst_ref=slot(k, me),
            send_sem=mate_send.at[k], recv_sem=mate_recv.at[k],
            device_id={"occ": mate}, device_id_type=MESH,
        )

    def forward(k, d):
        source = peer(n - 2 * d)
        return pltpu.make_async_remote_copy(
            src_ref=slot(k, source), dst_ref=slot(k, source),
            send_sem=fwd_send.at[d - 1, k], recv_sem=fwd_recv.at[d - 1, k],
            device_id={"occ": mate}, device_id_type=MESH,
        )

    def box(d):
        target = peer(d)
        return pltpu.make_async_remote_copy(
            src_ref=outbox.at[target], dst_ref=inbox.at[me],
            send_sem=box_send.at[d - 1], recv_sem=box_recv.at[d - 1],
            device_id={"occ": target}, device_id_type=MESH,
        )

    def code(d):
        target = peer(d)
        return pltpu.make_async_remote_copy(
            src_ref=code_out.at[target], dst_ref=code_in.at[me],
            send_sem=code_send.at[d - 1], recv_sem=code_recv.at[d - 1],
            device_id={"occ": target}, device_id_type=MESH,
        )

    @pl.loop(0, chunks)
    def _(k):
        load(k).start()

    fetch_amp = pltpu.make_async_copy(amp_hbm, amp, amp_sem)
    fetch_amp.start()

    barrier = pltpu.get_barrier_semaphore()
    for d in range(1, n):
        pl.semaphore_signal(barrier, inc=1, device_id={"occ": peer(d)}, device_id_type=MESH)
    pl.semaphore_wait(barrier, n - 1)

    col_tiles = mask_ref.shape[1]

    def send_chunk(k):
        tile_of = (k * CHUNK + lax.broadcasted_iota(jnp.int32, (col_tiles, CHUNK), 1)) // width
        spread = (tile_of == lax.broadcasted_iota(jnp.int32, (col_tiles, CHUNK), 0))
        kept = jnp.dot(
            mask_ref[...].astype(jnp.float32).astype(jnp.bfloat16),
            spread.astype(jnp.float32).astype(jnp.bfloat16),
            preferred_element_type=jnp.float32,
        ).astype(jnp.bfloat16)
        load(k).wait()
        for b in range(local_blocks):
            rows = pl.ds(pl.multiple_of(me * depth + b * width, width), width)
            gathered[k, rows, :] = gathered[k, rows, :] * kept[b : b + 1, :]
        for d in range(1, ranks_of_chips):
            far(k, d).start()
        near(k).start()

    early = min(EARLY, chunks)

    @pl.loop(0, early)
    def _(k):
        send_chunk(k)

    owner = owner_ref[...]
    tile_lane = lax.broadcasted_iota(jnp.int32, (tiles, tiles), 1)
    tile_sub = lax.broadcasted_iota(jnp.int32, (tiles, tiles), 0)
    owner_col = jnp.sum(
        jnp.where(tile_lane == tile_sub, jnp.broadcast_to(owner, (tiles, tiles)), 0),
        axis=1, keepdims=True,
    )
    same = (owner_col == owner) & (tile_sub < tile_lane)
    before = jnp.sum(same.astype(jnp.int32), axis=0, keepdims=True)
    tile_code = row_ref[...] * blocks + block_ref[...] + 1
    fetch_amp.wait()
    slot_sub = lax.rem(lax.broadcasted_iota(jnp.int32, (2 * capacity, tiles), 0), capacity)
    for o in range(n):
        chosen = (owner == o) & (before == slot_sub)
        picked = jnp.dot(
            chosen[:capacity].astype(jnp.float32).astype(jnp.bfloat16), amp[...],
            preferred_element_type=jnp.float32,
        )
        outbox[o] = jnp.concatenate([picked[:, :half], picked[:, half:]], axis=0).astype(jnp.bfloat16)
        code_col = jnp.sum(jnp.where(chosen, tile_code, 0), axis=1, keepdims=True)
        lane = lax.broadcasted_iota(jnp.int32, (2 * capacity, 128), 1)
        sub = lax.broadcasted_iota(jnp.int32, (2 * capacity, 128), 0)
        code_row = jnp.sum(jnp.where(lane == sub, code_col, 0), axis=0, keepdims=True)
        code_out[o] = jnp.broadcast_to(code_row, (8, 128))
    for d in range(1, n):
        box(d).start()
        code(d).start()

    @pl.loop(early, chunks)
    def _(k):
        send_chunk(k)

    inbox[me] = outbox[me]
    code_in[me] = code_out[me]
    for d in range(1, n):
        box(d).wait()
        code(d).wait()

    cell_sub = lax.broadcasted_iota(jnp.int32, (cells, 2 * capacity), 0)
    slot_half = lax.broadcasted_iota(jnp.int32, (cells, 2 * capacity), 1) // capacity
    ranks = rank_ref[...]
    rank_lane = lax.broadcasted_iota(jnp.int32, (cells, row_dev), 1)
    cell_row = lax.broadcasted_iota(jnp.int32, (cells, row_dev), 0) // blocks
    cell_rank = jnp.sum(jnp.where(rank_lane == cell_row, ranks, 0), axis=1, keepdims=True)
    per_half = half // 128

    for h in range(2):
        total = jnp.zeros((cells, half), jnp.float32)
        for o in range(n):
            here = (code_in[o][0:1, : 2 * capacity] == cell_sub + 1) & (slot_half == h)
            total = total + jnp.dot(
                here.astype(jnp.float32).astype(jnp.bfloat16), inbox[o],
                preferred_element_type=jnp.float32,
            )
        place = h * half + lax.broadcasted_iota(jnp.int32, (cells, half), 1)
        kept = (place // width < cell_rank) & (lax.rem(place, width) < cell_rank)
        total = jnp.where(kept, total, 0.0)
        for r in range(per_half):
            start = (h * per_half + r) * cells
            cells_s[start : start + cells, :] = total[:, r * 128 : (r + 1) * 128]

    pairs = width // 2
    low = lax.broadcasted_iota(jnp.int32, (pairs, 128), 1) < width
    for row in range(row_dev):
        @pl.loop(0, blocks // 2)
        def _(q):
            first = cells_s[pl.ds(row * blocks + 2 * q, pairs, stride=cells), :]
            second = cells_s[pl.ds(row * blocks + 2 * q + 1, pairs, stride=cells), :]
            even = jnp.where(low, first, pltpu.roll(second, width, 1))
            odd = jnp.where(low, pltpu.roll(first, width, 1), second)
            block_f32[q, pl.ds(row * width, pairs, stride=2), :] = even
            block_f32[q, pl.ds(row * width + 1, pairs, stride=2), :] = odd

    for q in range(blocks // 2):
        block_bf[:, q * 128 : (q + 1) * 128] = block_f32[q].astype(jnp.bfloat16)

    def store(k):
        return pltpu.make_async_copy(staged.at[k], out_hbm.at[:, columns(k)], out_sem.at[k])

    def multiply(k):
        near(k).wait_recv()
        for d in range(1, ranks_of_chips):
            forward(k, d).wait_recv()
        staged[k] = jnp.dot(
            block_bf[...], gathered[k], preferred_element_type=jnp.float32
        ).astype(jnp.bfloat16)
        store(k).start()

    def pass_on(k):
        for d in range(1, ranks_of_chips):
            far(k, d).wait_recv()
            forward(k, d).start()

    pass_on(0)

    @pl.loop(1, chunks)
    def _(k):
        pass_on(k)
        multiply(k - 1)

    multiply(chunks - 1)

    @pl.loop(0, chunks)
    def _(k):
        near(k).wait_send()
        for d in range(1, ranks_of_chips):
            far(k, d).wait_send()
            forward(k, d).wait_send()
        store(k).wait()


def body(amplitudes, panels, tile_mask, ranks, tile_owner, tile_row, tile_block):
    n = lax.axis_size("occ")
    tiles, flat = amplitudes.shape
    local_blocks, width, cols = panels.shape
    row_dev = ranks.shape[0]
    capacity = tiles // 4
    blocks = local_blocks * n
    depth = local_blocks * width
    chunks = cols // CHUNK
    others = n - 1
    chips = n // 2
    cells = row_dev * blocks
    whole = pl.BlockSpec(memory_space=pl.ANY)
    vmem = pl.BlockSpec(memory_space=pltpu.VMEM)
    dma = pltpu.SemaphoreType.DMA
    out = pl.pallas_call(
        functools.partial(kernel, n, row_dev, width, capacity),
        out_shape=jax.ShapeDtypeStruct((row_dev * width, cols), jnp.bfloat16),
        in_specs=[whole, whole] + [vmem] * 5,
        out_specs=whole,
        scratch_shapes=[
            pltpu.VMEM((chunks, blocks * width, CHUNK), jnp.bfloat16),
            pltpu.VMEM((tiles, flat), jnp.bfloat16),
            pltpu.VMEM((n, 2 * capacity, flat // 2), jnp.bfloat16),
            pltpu.VMEM((n, 2 * capacity, flat // 2), jnp.bfloat16),
            pltpu.VMEM((n, 8, 128), jnp.int32),
            pltpu.VMEM((n, 8, 128), jnp.int32),
            pltpu.VMEM((flat // 128 * cells, 128), jnp.float32),
            pltpu.VMEM((blocks // 2, row_dev * width, 128), jnp.float32),
            pltpu.VMEM((row_dev * width, blocks * width), jnp.bfloat16),
            pltpu.VMEM((chunks, row_dev * width, CHUNK), jnp.bfloat16),
            dma((chunks,)), dma,
            dma((chips - 1, chunks)), dma((chips - 1, chunks)),
            dma((chunks,)), dma((chunks,)),
            dma((chips - 1, chunks)), dma((chips - 1, chunks)),
            dma((others,)), dma((others,)), dma((others,)), dma((others,)),
            dma((chunks,)),
        ],
        compiler_params=pltpu.CompilerParams(
            collective_id=0, has_side_effects=True, vmem_limit_bytes=56 * 1024 * 1024
        ),
    )(
        panels.reshape(depth, cols), amplitudes, tile_mask, ranks[None], tile_owner[None],
        tile_row[None], tile_block[None],
    )
    return out.reshape(row_dev, width, cols)


def solution(mesh):
    placed = (
        P(("frag", "occ"), None),
        P(("frag", "occ"), None, "vir"),
        P(("frag", "occ"), "vir"),
        P(("frag", "occ")),
        P(("frag", "occ")),
        P(("frag", "occ")),
        P(("frag", "occ")),
    )
    return jax.shard_map(
        body, mesh=mesh, in_specs=placed, out_specs=P(("frag", "occ"), None, "vir"), check_vma=False
    )
```

```python
import functools

import jax
import jax.numpy as jnp
from jax import lax
from jax.experimental import pallas as pl
from jax.experimental.pallas import tpu as pltpu
from jax.sharding import PartitionSpec as P

MESH = pl.DeviceIdType.MESH
CHUNK = 256
EARLY = 4
VMEM_LIMIT = 59 * 1024 * 1024


def kernel(
    n, row_dev, width, capacity,
    panel_hbm, amp_hbm, mask_ref, rank_ref, owner_ref, row_ref, block_ref,
    out_ref,
    gathered, amp, outbox, inbox, code_out, code_in, cells_s, block_f32, block_bf,
    load_sem, amp_sem, far_send, far_recv, mate_send, mate_recv, fwd_send, fwd_recv,
    box_send, box_recv, code_send, code_recv,
):
    me = lax.axis_index("occ")
    ranks_of_chips = n // 2
    mate = me + 1 - 2 * lax.rem(me, 2)
    chunks = gathered.shape[0]
    depth = panel_hbm.shape[0]
    local_blocks = depth // width
    blocks = local_blocks * n
    tiles = amp.shape[0]
    flat = amp.shape[1]
    half = flat // 2
    cells = row_dev * blocks

    def peer(distance):
        return lax.rem(me + distance, n)

    def slot(k, source):
        return gathered.at[k, pl.ds(pl.multiple_of(source * depth, depth), depth), :]

    def columns(k):
        return pl.ds(pl.multiple_of(k * CHUNK, CHUNK), CHUNK)

    def load(k):
        return pltpu.make_async_copy(panel_hbm.at[:, columns(k)], slot(k, me), load_sem.at[k])

    def far(k, d):
        return pltpu.make_async_remote_copy(
            src_ref=slot(k, me), dst_ref=slot(k, me),
            send_sem=far_send.at[d - 1, k], recv_sem=far_recv.at[d - 1, k],
            device_id={"occ": peer(2 * d)}, device_id_type=MESH,
        )

    def near(k):
        return pltpu.make_async_remote_copy(
            src_ref=slot(k, me), dst_ref=slot(k, me),
            send_sem=mate_send.at[k], recv_sem=mate_recv.at[k],
            device_id={"occ": mate}, device_id_type=MESH,
        )

    def forward(k, d):
        source = peer(n - 2 * d)
        return pltpu.make_async_remote_copy(
            src_ref=slot(k, source), dst_ref=slot(k, source),
            send_sem=fwd_send.at[d - 1, k], recv_sem=fwd_recv.at[d - 1, k],
            device_id={"occ": mate}, device_id_type=MESH,
        )

    def box(d):
        target = peer(d)
        return pltpu.make_async_remote_copy(
            src_ref=outbox.at[target], dst_ref=inbox.at[me],
            send_sem=box_send.at[d - 1], recv_sem=box_recv.at[d - 1],
            device_id={"occ": target}, device_id_type=MESH,
        )

    def code(d):
        target = peer(d)
        return pltpu.make_async_remote_copy(
            src_ref=code_out.at[target], dst_ref=code_in.at[me],
            send_sem=code_send.at[d - 1], recv_sem=code_recv.at[d - 1],
            device_id={"occ": target}, device_id_type=MESH,
        )

    barrier = pltpu.get_barrier_semaphore()
    for d in range(1, n):
        pl.semaphore_signal(barrier, inc=1, device_id={"occ": peer(d)}, device_id_type=MESH)

    @pl.loop(0, chunks)
    def _(k):
        load(k).start()

    fetch_amp = pltpu.make_async_copy(amp_hbm, amp, amp_sem)
    fetch_amp.start()

    col_tiles = mask_ref.shape[1]

    def mask_chunk(k):
        tile_of = (k * CHUNK + lax.broadcasted_iota(jnp.int32, (col_tiles, CHUNK), 1)) // width
        spread = (tile_of == lax.broadcasted_iota(jnp.int32, (col_tiles, CHUNK), 0))
        kept = jnp.dot(
            mask_ref[...].astype(jnp.float32).astype(jnp.bfloat16),
            spread.astype(jnp.float32).astype(jnp.bfloat16),
            preferred_element_type=jnp.float32,
        ).astype(jnp.bfloat16)
        load(k).wait()
        for b in range(local_blocks):
            rows = pl.ds(pl.multiple_of(me * depth + b * width, width), width)
            gathered[k, rows, :] = gathered[k, rows, :] * kept[b : b + 1, :]

    def send_chunk(k):
        for d in range(1, ranks_of_chips):
            far(k, d).start()
        near(k).start()

    early = min(EARLY, chunks)

    mask_chunk(0)
    pl.semaphore_wait(barrier, n - 1)
    send_chunk(0)

    @pl.loop(1, early)
    def _(k):
        mask_chunk(k)
        send_chunk(k)

    owner = owner_ref[...]
    tile_lane = lax.broadcasted_iota(jnp.int32, (tiles, tiles), 1)
    tile_sub = lax.broadcasted_iota(jnp.int32, (tiles, tiles), 0)
    owner_col = jnp.sum(
        jnp.where(tile_lane == tile_sub, jnp.broadcast_to(owner, (tiles, tiles)), 0),
        axis=1, keepdims=True,
    )
    same = (owner_col == owner) & (tile_sub < tile_lane)
    before = jnp.sum(same.astype(jnp.int32), axis=0, keepdims=True)
    tile_code = row_ref[...] * blocks + block_ref[...] + 1
    fetch_amp.wait()
    slot_sub = lax.rem(lax.broadcasted_iota(jnp.int32, (2 * capacity, tiles), 0), capacity)
    for o in range(n):
        chosen = (owner == o) & (before == slot_sub)
        picked = jnp.dot(
            chosen[:capacity].astype(jnp.float32).astype(jnp.bfloat16), amp[...],
            preferred_element_type=jnp.float32,
        )
        outbox[o] = jnp.concatenate([picked[:, :half], picked[:, half:]], axis=0).astype(jnp.bfloat16)
        code_col = jnp.sum(jnp.where(chosen, tile_code, 0), axis=1, keepdims=True)
        lane = lax.broadcasted_iota(jnp.int32, (2 * capacity, 128), 1)
        sub = lax.broadcasted_iota(jnp.int32, (2 * capacity, 128), 0)
        code_row = jnp.sum(jnp.where(lane == sub, code_col, 0), axis=0, keepdims=True)
        code_out[o] = jnp.broadcast_to(code_row, (8, 128))
    for d in range(1, n):
        box(d).start()
        code(d).start()

    @pl.loop(early, chunks)
    def _(k):
        mask_chunk(k)
        send_chunk(k)

    inbox[me] = outbox[me]
    code_in[me] = code_out[me]
    for d in range(1, n):
        box(d).wait()
        code(d).wait()

    cell_sub = lax.broadcasted_iota(jnp.int32, (cells, 2 * capacity), 0)
    slot_half = lax.broadcasted_iota(jnp.int32, (cells, 2 * capacity), 1) // capacity
    ranks = rank_ref[...]
    rank_lane = lax.broadcasted_iota(jnp.int32, (cells, row_dev), 1)
    cell_row = lax.broadcasted_iota(jnp.int32, (cells, row_dev), 0) // blocks
    cell_rank = jnp.sum(jnp.where(rank_lane == cell_row, ranks, 0), axis=1, keepdims=True)
    per_half = half // 128

    for h in range(2):
        total = jnp.zeros((cells, half), jnp.float32)
        for o in range(n):
            here = (code_in[o][0:1, : 2 * capacity] == cell_sub + 1) & (slot_half == h)
            total = total + jnp.dot(
                here.astype(jnp.float32).astype(jnp.bfloat16), inbox[o],
                preferred_element_type=jnp.float32,
            )
        place = h * half + lax.broadcasted_iota(jnp.int32, (cells, half), 1)
        kept = (place // width < cell_rank) & (lax.rem(place, width) < cell_rank)
        total = jnp.where(kept, total, 0.0)
        for r in range(per_half):
            start = (h * per_half + r) * cells
            cells_s[start : start + cells, :] = total[:, r * 128 : (r + 1) * 128]

    pairs = width // 2
    low = lax.broadcasted_iota(jnp.int32, (pairs, 128), 1) < width
    for row in range(row_dev):
        @pl.loop(0, blocks // 2)
        def _(q):
            first = cells_s[pl.ds(row * blocks + 2 * q, pairs, stride=cells), :]
            second = cells_s[pl.ds(row * blocks + 2 * q + 1, pairs, stride=cells), :]
            even = jnp.where(low, first, pltpu.roll(second, width, 1))
            odd = jnp.where(low, pltpu.roll(first, width, 1), second)
            block_f32[q, pl.ds(row * width, pairs, stride=2), :] = even
            block_f32[q, pl.ds(row * width + 1, pairs, stride=2), :] = odd

    for q in range(blocks // 2):
        block_bf[:, q * 128 : (q + 1) * 128] = block_f32[q].astype(jnp.bfloat16)

    def multiply(k):
        near(k).wait_recv()
        for d in range(1, ranks_of_chips):
            forward(k, d).wait_recv()
        out_ref[k] = jnp.dot(
            block_bf[...], gathered[k], preferred_element_type=jnp.float32
        ).astype(jnp.bfloat16)

    def pass_on(k):
        for d in range(1, ranks_of_chips):
            far(k, d).wait_recv()
            forward(k, d).start()

    pass_on(0)

    @pl.loop(1, chunks)
    def _(k):
        pass_on(k)
        multiply(k - 1)

    multiply(chunks - 1)

    @pl.loop(0, chunks)
    def _(k):
        near(k).wait_send()
        for d in range(1, ranks_of_chips):
            far(k, d).wait_send()
            forward(k, d).wait_send()


def write_kernel(held, out_hbm, out_sem):
    chunks = held.shape[0]

    def store(k):
        place = pl.ds(pl.multiple_of(k * CHUNK, CHUNK), CHUNK)
        return pltpu.make_async_copy(held.at[k], out_hbm.at[:, place], out_sem.at[k])

    @pl.loop(0, chunks)
    def _(k):
        store(k).start()

    @pl.loop(0, chunks)
    def _(k):
        store(k).wait()


def body(amplitudes, panels, tile_mask, ranks, tile_owner, tile_row, tile_block):
    n = lax.axis_size("occ")
    tiles, flat = amplitudes.shape
    local_blocks, width, cols = panels.shape
    row_dev = ranks.shape[0]
    capacity = tiles // 4
    blocks = local_blocks * n
    depth = local_blocks * width
    chunks = cols // CHUNK
    others = n - 1
    chips = n // 2
    cells = row_dev * blocks
    whole = pl.BlockSpec(memory_space=pl.ANY)
    vmem = pl.BlockSpec(memory_space=pltpu.VMEM)
    dma = pltpu.SemaphoreType.DMA
    out = pl.pallas_call(
        functools.partial(kernel, n, row_dev, width, capacity),
        out_shape=pltpu.VMEM((chunks, row_dev * width, CHUNK), jnp.bfloat16),
        in_specs=[whole, whole] + [vmem] * 5,
        out_specs=vmem,
        scratch_shapes=[
            pltpu.VMEM((chunks, blocks * width, CHUNK), jnp.bfloat16),
            pltpu.VMEM((tiles, flat), jnp.bfloat16),
            pltpu.VMEM((n, 2 * capacity, flat // 2), jnp.bfloat16),
            pltpu.VMEM((n, 2 * capacity, flat // 2), jnp.bfloat16),
            pltpu.VMEM((n, 8, 128), jnp.int32),
            pltpu.VMEM((n, 8, 128), jnp.int32),
            pltpu.VMEM((flat // 128 * cells, 128), jnp.float32),
            pltpu.VMEM((blocks // 2, row_dev * width, 128), jnp.float32),
            pltpu.VMEM((row_dev * width, blocks * width), jnp.bfloat16),
            dma((chunks,)), dma,
            dma((chips - 1, chunks)), dma((chips - 1, chunks)),
            dma((chunks,)), dma((chunks,)),
            dma((chips - 1, chunks)), dma((chips - 1, chunks)),
            dma((others,)), dma((others,)), dma((others,)), dma((others,)),
        ],
        compiler_params=pltpu.CompilerParams(
            collective_id=0, has_side_effects=True, vmem_limit_bytes=VMEM_LIMIT
        ),
    )(
        panels.reshape(depth, cols), amplitudes, tile_mask, ranks[None], tile_owner[None],
        tile_row[None], tile_block[None],
    )
    return pl.pallas_call(
        write_kernel,
        out_shape=jax.ShapeDtypeStruct((row_dev * width, cols), jnp.bfloat16),
        in_specs=[vmem],
        out_specs=whole,
        scratch_shapes=[dma((chunks,))],
    )(out).reshape(row_dev, width, cols)


def solution(mesh):
    placed = (
        P(("frag", "occ"), None),
        P(("frag", "occ"), None, "vir"),
        P(("frag", "occ"), "vir"),
        P(("frag", "occ")),
        P(("frag", "occ")),
        P(("frag", "occ")),
        P(("frag", "occ")),
    )
    return jax.shard_map(
        body, mesh=mesh, in_specs=placed, out_specs=P(("frag", "occ"), None, "vir"), check_vma=False
    )
```

```python
import functools

import jax
import jax.numpy as jnp
from jax import lax
from jax.experimental import pallas as pl
from jax.experimental.pallas import tpu as pltpu
from jax.sharding import PartitionSpec as P

MESH = pl.DeviceIdType.MESH
CHUNK = 256
EARLY = 4
PARTS = 4
VMEM_LIMIT = 59 * 1024 * 1024


def kernel(
    n, row_dev, width, capacity,
    panel_hbm, amp_hbm, mask_hbm, rank_hbm, owner_hbm, row_hbm, block_hbm,
    out_ref,
    gathered, amp, outbox, inbox, code_out, code_in, cells_s, block_f32, block_bf,
    mask_ref, rank_ref, owner_ref, row_ref, block_ref, small_sem,
    load_sem, amp_sem, far_send, far_recv, mate_send, mate_recv, fwd_send, fwd_recv,
    box_send, box_recv, code_send, code_recv,
):
    me = lax.axis_index("occ")
    ranks_of_chips = n // 2
    mate = me + 1 - 2 * lax.rem(me, 2)
    chunks = gathered.shape[0]
    depth = panel_hbm.shape[0]
    local_blocks = depth // width
    blocks = local_blocks * n
    tiles = amp.shape[0]
    flat = amp.shape[1]
    half = flat // 2
    cells = row_dev * blocks

    def peer(distance):
        return lax.rem(me + distance, n)

    def slot(k, source):
        return gathered.at[k, pl.ds(pl.multiple_of(source * depth, depth), depth), :]

    def columns(k):
        return pl.ds(pl.multiple_of(k * CHUNK, CHUNK), CHUNK)

    def load(k):
        return pltpu.make_async_copy(panel_hbm.at[:, columns(k)], slot(k, me), load_sem.at[k])

    def far(k, d):
        return pltpu.make_async_remote_copy(
            src_ref=slot(k, me), dst_ref=slot(k, me),
            send_sem=far_send.at[d - 1, k], recv_sem=far_recv.at[d - 1, k],
            device_id={"occ": peer(2 * d)}, device_id_type=MESH,
        )

    def near(k):
        return pltpu.make_async_remote_copy(
            src_ref=slot(k, me), dst_ref=slot(k, me),
            send_sem=mate_send.at[k], recv_sem=mate_recv.at[k],
            device_id={"occ": mate}, device_id_type=MESH,
        )

    def forward(k, d):
        source = peer(n - 2 * d)
        return pltpu.make_async_remote_copy(
            src_ref=slot(k, source), dst_ref=slot(k, source),
            send_sem=fwd_send.at[d - 1, k], recv_sem=fwd_recv.at[d - 1, k],
            device_id={"occ": mate}, device_id_type=MESH,
        )

    def box(d):
        target = peer(d)
        return pltpu.make_async_remote_copy(
            src_ref=outbox.at[target], dst_ref=inbox.at[me],
            send_sem=box_send.at[d - 1], recv_sem=box_recv.at[d - 1],
            device_id={"occ": target}, device_id_type=MESH,
        )

    def code(d):
        target = peer(d)
        return pltpu.make_async_remote_copy(
            src_ref=code_out.at[target], dst_ref=code_in.at[me],
            send_sem=code_send.at[d - 1], recv_sem=code_recv.at[d - 1],
            device_id={"occ": target}, device_id_type=MESH,
        )

    barrier = pltpu.get_barrier_semaphore()
    for d in range(1, n):
        pl.semaphore_signal(barrier, inc=1, device_id={"occ": peer(d)}, device_id_type=MESH)

    small = [
        pltpu.make_async_copy(source, target, small_sem.at[i])
        for i, (source, target) in enumerate((
            (mask_hbm, mask_ref), (rank_hbm, rank_ref), (owner_hbm, owner_ref),
            (row_hbm, row_ref), (block_hbm, block_ref),
        ))
    ]
    load(0).start()
    for copy in small:
        copy.start()

    @pl.loop(1, chunks)
    def _(k):
        load(k).start()

    fetch_amp = pltpu.make_async_copy(amp_hbm, amp, amp_sem)
    fetch_amp.start()

    col_tiles = mask_ref.shape[1]

    def mask_chunk(k):
        tile_of = (k * CHUNK + lax.broadcasted_iota(jnp.int32, (col_tiles, CHUNK), 1)) // width
        spread = (tile_of == lax.broadcasted_iota(jnp.int32, (col_tiles, CHUNK), 0))
        kept = jnp.dot(
            mask_ref[...].astype(jnp.float32).astype(jnp.bfloat16),
            spread.astype(jnp.float32).astype(jnp.bfloat16),
            preferred_element_type=jnp.float32,
        ).astype(jnp.bfloat16)
        load(k).wait()
        for b in range(local_blocks):
            rows = pl.ds(pl.multiple_of(me * depth + b * width, width), width)
            gathered[k, rows, :] = gathered[k, rows, :] * kept[b : b + 1, :]

    def send_chunk(k):
        for d in range(1, ranks_of_chips):
            far(k, d).start()
        near(k).start()

    early = min(EARLY, chunks)

    for copy in small:
        copy.wait()
    mask_chunk(0)
    pl.semaphore_wait(barrier, n - 1)
    send_chunk(0)

    @pl.loop(1, early)
    def _(k):
        mask_chunk(k)
        send_chunk(k)

    owner = owner_ref[...]
    tile_lane = lax.broadcasted_iota(jnp.int32, (tiles, tiles), 1)
    tile_sub = lax.broadcasted_iota(jnp.int32, (tiles, tiles), 0)
    owner_col = jnp.sum(
        jnp.where(tile_lane == tile_sub, jnp.broadcast_to(owner, (tiles, tiles)), 0),
        axis=1, keepdims=True,
    )
    same = (owner_col == owner) & (tile_sub < tile_lane)
    before = jnp.sum(same.astype(jnp.int32), axis=0, keepdims=True)
    tile_code = row_ref[...] * blocks + block_ref[...] + 1
    fetch_amp.wait()
    slot_sub = lax.rem(lax.broadcasted_iota(jnp.int32, (2 * capacity, tiles), 0), capacity)
    for o in range(n):
        chosen = (owner == o) & (before == slot_sub)
        picked = jnp.dot(
            chosen[:capacity].astype(jnp.float32).astype(jnp.bfloat16), amp[...],
            preferred_element_type=jnp.float32,
        )
        outbox[o] = jnp.concatenate([picked[:, :half], picked[:, half:]], axis=0).astype(jnp.bfloat16)
        code_col = jnp.sum(jnp.where(chosen, tile_code, 0), axis=1, keepdims=True)
        lane = lax.broadcasted_iota(jnp.int32, (2 * capacity, 128), 1)
        sub = lax.broadcasted_iota(jnp.int32, (2 * capacity, 128), 0)
        code_row = jnp.sum(jnp.where(lane == sub, code_col, 0), axis=0, keepdims=True)
        code_out[o] = jnp.broadcast_to(code_row, (8, 128))
    for d in range(1, n):
        box(d).start()
        code(d).start()

    @pl.loop(early, chunks)
    def _(k):
        mask_chunk(k)
        send_chunk(k)

    inbox[me] = outbox[me]
    code_in[me] = code_out[me]
    for d in range(1, n):
        box(d).wait()
        code(d).wait()

    cell_sub = lax.broadcasted_iota(jnp.int32, (cells, 2 * capacity), 0)
    slot_half = lax.broadcasted_iota(jnp.int32, (cells, 2 * capacity), 1) // capacity
    ranks = rank_ref[...]
    rank_lane = lax.broadcasted_iota(jnp.int32, (cells, row_dev), 1)
    cell_row = lax.broadcasted_iota(jnp.int32, (cells, row_dev), 0) // blocks
    cell_rank = jnp.sum(jnp.where(rank_lane == cell_row, ranks, 0), axis=1, keepdims=True)
    per_half = half // 128

    for h in range(2):
        total = jnp.zeros((cells, half), jnp.float32)
        for o in range(n):
            here = (code_in[o][0:1, : 2 * capacity] == cell_sub + 1) & (slot_half == h)
            total = total + jnp.dot(
                here.astype(jnp.float32).astype(jnp.bfloat16), inbox[o],
                preferred_element_type=jnp.float32,
            )
        place = h * half + lax.broadcasted_iota(jnp.int32, (cells, half), 1)
        kept = (place // width < cell_rank) & (lax.rem(place, width) < cell_rank)
        total = jnp.where(kept, total, 0.0)
        for r in range(per_half):
            start = (h * per_half + r) * cells
            cells_s[start : start + cells, :] = total[:, r * 128 : (r + 1) * 128]

    pairs = width // 2
    low = lax.broadcasted_iota(jnp.int32, (pairs, 128), 1) < width
    for row in range(row_dev):
        @pl.loop(0, blocks // 2)
        def _(q):
            first = cells_s[pl.ds(row * blocks + 2 * q, pairs, stride=cells), :]
            second = cells_s[pl.ds(row * blocks + 2 * q + 1, pairs, stride=cells), :]
            even = jnp.where(low, first, pltpu.roll(second, width, 1))
            odd = jnp.where(low, pltpu.roll(first, width, 1), second)
            block_f32[q, pl.ds(row * width, pairs, stride=2), :] = even
            block_f32[q, pl.ds(row * width + 1, pairs, stride=2), :] = odd

    for q in range(blocks // 2):
        block_bf[:, q * 128 : (q + 1) * 128] = block_f32[q].astype(jnp.bfloat16)

    def multiply(k):
        near(k).wait_recv()
        for d in range(1, ranks_of_chips):
            forward(k, d).wait_recv()
        out_ref[:, columns(k)] = jnp.dot(
            block_bf[...], gathered[k], preferred_element_type=jnp.float32
        ).astype(jnp.bfloat16)

    def pass_on(k):
        for d in range(1, ranks_of_chips):
            far(k, d).wait_recv()
            forward(k, d).start()

    pass_on(0)

    @pl.loop(1, chunks)
    def _(k):
        pass_on(k)
        multiply(k - 1)

    multiply(chunks - 1)

    @pl.loop(0, chunks)
    def _(k):
        near(k).wait_send()
        for d in range(1, ranks_of_chips):
            far(k, d).wait_send()
            forward(k, d).wait_send()


def write_kernel(held, out_hbm, out_sem):
    parts = out_sem.shape[0]
    rows = held.shape[0] // parts

    def store(k):
        place = pl.ds(k * rows, rows)
        return pltpu.make_async_copy(held.at[place, :], out_hbm.at[place, :], out_sem.at[k])

    for k in range(parts):
        store(k).start()
    for k in range(parts):
        store(k).wait()


def body(amplitudes, panels, tile_mask, ranks, tile_owner, tile_row, tile_block):
    n = lax.axis_size("occ")
    tiles, flat = amplitudes.shape
    local_blocks, width, cols = panels.shape
    row_dev = ranks.shape[0]
    capacity = tiles // 4
    blocks = local_blocks * n
    depth = local_blocks * width
    chunks = cols // CHUNK
    others = n - 1
    chips = n // 2
    cells = row_dev * blocks
    whole = pl.BlockSpec(memory_space=pl.ANY)
    vmem = pl.BlockSpec(memory_space=pltpu.VMEM)
    dma = pltpu.SemaphoreType.DMA
    out = pl.pallas_call(
        functools.partial(kernel, n, row_dev, width, capacity),
        out_shape=pltpu.VMEM((row_dev * width, cols), jnp.bfloat16),
        in_specs=[whole] * 7,
        out_specs=vmem,
        scratch_shapes=[
            pltpu.VMEM((chunks, blocks * width, CHUNK), jnp.bfloat16),
            pltpu.VMEM((tiles, flat), jnp.bfloat16),
            pltpu.VMEM((n, 2 * capacity, flat // 2), jnp.bfloat16),
            pltpu.VMEM((n, 2 * capacity, flat // 2), jnp.bfloat16),
            pltpu.VMEM((n, 8, 128), jnp.int32),
            pltpu.VMEM((n, 8, 128), jnp.int32),
            pltpu.VMEM((flat // 128 * cells, 128), jnp.float32),
            pltpu.VMEM((blocks // 2, row_dev * width, 128), jnp.float32),
            pltpu.VMEM((row_dev * width, blocks * width), jnp.bfloat16),
            pltpu.VMEM((local_blocks, cols // width), jnp.int32),
            pltpu.VMEM((1, row_dev), jnp.int32),
            pltpu.VMEM((1, tiles), jnp.int32),
            pltpu.VMEM((1, tiles), jnp.int32),
            pltpu.VMEM((1, tiles), jnp.int32),
            dma((5,)),
            dma((chunks,)), dma,
            dma((chips - 1, chunks)), dma((chips - 1, chunks)),
            dma((chunks,)), dma((chunks,)),
            dma((chips - 1, chunks)), dma((chips - 1, chunks)),
            dma((others,)), dma((others,)), dma((others,)), dma((others,)),
        ],
        compiler_params=pltpu.CompilerParams(
            collective_id=0, has_side_effects=True, vmem_limit_bytes=VMEM_LIMIT
        ),
    )(
        panels.reshape(depth, cols), amplitudes, tile_mask, ranks[None], tile_owner[None],
        tile_row[None], tile_block[None],
    )
    return pl.pallas_call(
        write_kernel,
        out_shape=jax.ShapeDtypeStruct((row_dev * width, cols), jnp.bfloat16),
        in_specs=[vmem],
        out_specs=whole,
        scratch_shapes=[dma((PARTS,))],
        compiler_params=pltpu.CompilerParams(vmem_limit_bytes=1024 * 1024),
    )(out).reshape(row_dev, width, cols)


def solution(mesh):
    placed = (
        P(("frag", "occ"), None),
        P(("frag", "occ"), None, "vir"),
        P(("frag", "occ"), "vir"),
        P(("frag", "occ")),
        P(("frag", "occ")),
        P(("frag", "occ")),
        P(("frag", "occ")),
    )
    return jax.shard_map(
        body, mesh=mesh, in_specs=placed, out_specs=P(("frag", "occ"), None, "vir"), check_vma=False
    )
```

```python
import functools

import jax
import jax.numpy as jnp
from jax import lax
from jax.experimental import pallas as pl
from jax.experimental.pallas import tpu as pltpu
from jax.sharding import PartitionSpec as P

MESH = pl.DeviceIdType.MESH
CHUNK = 512
EARLY = 2
PARTS = 4
VMEM_LIMIT = 59 * 1024 * 1024


def kernel(
    n, row_dev, width, capacity,
    panel_hbm, amp_hbm, mask_hbm, rank_hbm, owner_hbm, row_hbm, block_hbm,
    out_ref,
    gathered, amp, outbox, inbox, code_out, code_in, cells_s, block_f32, block_bf,
    mask_ref, rank_ref, owner_ref, row_ref, block_ref, small_sem,
    load_sem, amp_sem, far_send, far_recv, mate_send, mate_recv, fwd_send, fwd_recv,
    box_send, box_recv, code_send, code_recv,
):
    me = lax.axis_index("occ")
    ranks_of_chips = n // 2
    mate = me + 1 - 2 * lax.rem(me, 2)
    chunks = gathered.shape[0]
    depth = panel_hbm.shape[0]
    local_blocks = depth // width
    blocks = local_blocks * n
    tiles = amp.shape[0]
    flat = amp.shape[1]
    half = flat // 2
    cells = row_dev * blocks

    def peer(distance):
        return lax.rem(me + distance, n)

    def slot(k, source):
        return gathered.at[k, pl.ds(pl.multiple_of(source * depth, depth), depth), :]

    def columns(k):
        return pl.ds(pl.multiple_of(k * CHUNK, CHUNK), CHUNK)

    def load(k):
        return pltpu.make_async_copy(panel_hbm.at[:, columns(k)], slot(k, me), load_sem.at[k])

    def far(k, d):
        return pltpu.make_async_remote_copy(
            src_ref=slot(k, me), dst_ref=slot(k, me),
            send_sem=far_send.at[d - 1, k], recv_sem=far_recv.at[d - 1, k],
            device_id={"occ": peer(2 * d)}, device_id_type=MESH,
        )

    def near(k):
        return pltpu.make_async_remote_copy(
            src_ref=slot(k, me), dst_ref=slot(k, me),
            send_sem=mate_send.at[k], recv_sem=mate_recv.at[k],
            device_id={"occ": mate}, device_id_type=MESH,
        )

    def forward(k, d):
        source = peer(n - 2 * d)
        return pltpu.make_async_remote_copy(
            src_ref=slot(k, source), dst_ref=slot(k, source),
            send_sem=fwd_send.at[d - 1, k], recv_sem=fwd_recv.at[d - 1, k],
            device_id={"occ": mate}, device_id_type=MESH,
        )

    def box(d):
        target = peer(d)
        return pltpu.make_async_remote_copy(
            src_ref=outbox.at[target], dst_ref=inbox.at[me],
            send_sem=box_send.at[d - 1], recv_sem=box_recv.at[d - 1],
            device_id={"occ": target}, device_id_type=MESH,
        )

    def code(d):
        target = peer(d)
        return pltpu.make_async_remote_copy(
            src_ref=code_out.at[target], dst_ref=code_in.at[me],
            send_sem=code_send.at[d - 1], recv_sem=code_recv.at[d - 1],
            device_id={"occ": target}, device_id_type=MESH,
        )

    barrier = pltpu.get_barrier_semaphore()
    for d in range(1, n):
        pl.semaphore_signal(barrier, inc=1, device_id={"occ": peer(d)}, device_id_type=MESH)

    small = [
        pltpu.make_async_copy(source, target, small_sem.at[i])
        for i, (source, target) in enumerate((
            (mask_hbm, mask_ref), (rank_hbm, rank_ref), (owner_hbm, owner_ref),
            (row_hbm, row_ref), (block_hbm, block_ref),
        ))
    ]
    load(0).start()
    for copy in small:
        copy.start()

    @pl.loop(1, chunks)
    def _(k):
        load(k).start()

    fetch_amp = pltpu.make_async_copy(amp_hbm, amp, amp_sem)
    fetch_amp.start()

    col_tiles = mask_ref.shape[1]

    def mask_chunk(k):
        tile_of = (k * CHUNK + lax.broadcasted_iota(jnp.int32, (col_tiles, CHUNK), 1)) // width
        spread = (tile_of == lax.broadcasted_iota(jnp.int32, (col_tiles, CHUNK), 0))
        kept = jnp.dot(
            mask_ref[...].astype(jnp.float32).astype(jnp.bfloat16),
            spread.astype(jnp.float32).astype(jnp.bfloat16),
            preferred_element_type=jnp.float32,
        ).astype(jnp.bfloat16)
        load(k).wait()
        for b in range(local_blocks):
            rows = pl.ds(pl.multiple_of(me * depth + b * width, width), width)
            gathered[k, rows, :] = gathered[k, rows, :] * kept[b : b + 1, :]

    def send_chunk(k):
        for d in range(1, ranks_of_chips):
            far(k, d).start()
        near(k).start()

    early = min(EARLY, chunks)

    for copy in small:
        copy.wait()
    mask_chunk(0)
    pl.semaphore_wait(barrier, n - 1)
    send_chunk(0)

    @pl.loop(1, early)
    def _(k):
        mask_chunk(k)
        send_chunk(k)

    owner = owner_ref[...]
    tile_lane = lax.broadcasted_iota(jnp.int32, (tiles, tiles), 1)
    tile_sub = lax.broadcasted_iota(jnp.int32, (tiles, tiles), 0)
    owner_col = jnp.sum(
        jnp.where(tile_lane == tile_sub, jnp.broadcast_to(owner, (tiles, tiles)), 0),
        axis=1, keepdims=True,
    )
    same = (owner_col == owner) & (tile_sub < tile_lane)
    before = jnp.sum(same.astype(jnp.int32), axis=0, keepdims=True)
    tile_code = row_ref[...] * blocks + block_ref[...] + 1
    fetch_amp.wait()
    slot_sub = lax.rem(lax.broadcasted_iota(jnp.int32, (2 * capacity, tiles), 0), capacity)
    for o in range(n):
        chosen = (owner == o) & (before == slot_sub)
        picked = jnp.dot(
            chosen[:capacity].astype(jnp.float32).astype(jnp.bfloat16), amp[...],
            preferred_element_type=jnp.float32,
        )
        outbox[o] = jnp.concatenate([picked[:, :half], picked[:, half:]], axis=0).astype(jnp.bfloat16)
        code_col = jnp.sum(jnp.where(chosen, tile_code, 0), axis=1, keepdims=True)
        lane = lax.broadcasted_iota(jnp.int32, (2 * capacity, 128), 1)
        sub = lax.broadcasted_iota(jnp.int32, (2 * capacity, 128), 0)
        code_row = jnp.sum(jnp.where(lane == sub, code_col, 0), axis=0, keepdims=True)
        code_out[o] = jnp.broadcast_to(code_row, (8, 128))
    for d in range(1, n):
        box(d).start()
        code(d).start()

    @pl.loop(early, chunks)
    def _(k):
        mask_chunk(k)
        send_chunk(k)

    inbox[me] = outbox[me]
    code_in[me] = code_out[me]
    for d in range(1, n):
        box(d).wait()
        code(d).wait()

    cell_sub = lax.broadcasted_iota(jnp.int32, (cells, 2 * capacity), 0)
    slot_half = lax.broadcasted_iota(jnp.int32, (cells, 2 * capacity), 1) // capacity
    ranks = rank_ref[...]
    rank_lane = lax.broadcasted_iota(jnp.int32, (cells, row_dev), 1)
    cell_row = lax.broadcasted_iota(jnp.int32, (cells, row_dev), 0) // blocks
    cell_rank = jnp.sum(jnp.where(rank_lane == cell_row, ranks, 0), axis=1, keepdims=True)
    per_half = half // 128

    for h in range(2):
        total = jnp.zeros((cells, half), jnp.float32)
        for o in range(n):
            here = (code_in[o][0:1, : 2 * capacity] == cell_sub + 1) & (slot_half == h)
            total = total + jnp.dot(
                here.astype(jnp.float32).astype(jnp.bfloat16), inbox[o],
                preferred_element_type=jnp.float32,
            )
        place = h * half + lax.broadcasted_iota(jnp.int32, (cells, half), 1)
        kept = (place // width < cell_rank) & (lax.rem(place, width) < cell_rank)
        total = jnp.where(kept, total, 0.0)
        for r in range(per_half):
            start = (h * per_half + r) * cells
            cells_s[start : start + cells, :] = total[:, r * 128 : (r + 1) * 128]

    pairs = width // 2
    low = lax.broadcasted_iota(jnp.int32, (pairs, 128), 1) < width
    for row in range(row_dev):
        @pl.loop(0, blocks // 2)
        def _(q):
            first = cells_s[pl.ds(row * blocks + 2 * q, pairs, stride=cells), :]
            second = cells_s[pl.ds(row * blocks + 2 * q + 1, pairs, stride=cells), :]
            even = jnp.where(low, first, pltpu.roll(second, width, 1))
            odd = jnp.where(low, pltpu.roll(first, width, 1), second)
            block_f32[q, pl.ds(row * width, pairs, stride=2), :] = even
            block_f32[q, pl.ds(row * width + 1, pairs, stride=2), :] = odd

    for q in range(blocks // 2):
        block_bf[:, q * 128 : (q + 1) * 128] = block_f32[q].astype(jnp.bfloat16)

    def multiply(k):
        near(k).wait_recv()
        for d in range(1, ranks_of_chips):
            forward(k, d).wait_recv()
        out_ref[:, columns(k)] = jnp.dot(
            block_bf[...], gathered[k], preferred_element_type=jnp.float32
        ).astype(jnp.bfloat16)

    def pass_on(k):
        for d in range(1, ranks_of_chips):
            far(k, d).wait_recv()
            forward(k, d).start()

    pass_on(0)

    @pl.loop(1, chunks)
    def _(k):
        pass_on(k)
        multiply(k - 1)

    multiply(chunks - 1)

    @pl.loop(0, chunks)
    def _(k):
        near(k).wait_send()
        for d in range(1, ranks_of_chips):
            far(k, d).wait_send()
            forward(k, d).wait_send()


def write_kernel(held, out_hbm, out_sem):
    parts = out_sem.shape[0]
    rows = held.shape[0] // parts

    def store(k):
        place = pl.ds(k * rows, rows)
        return pltpu.make_async_copy(held.at[place, :], out_hbm.at[place, :], out_sem.at[k])

    for k in range(parts):
        store(k).start()
    for k in range(parts):
        store(k).wait()


def body(amplitudes, panels, tile_mask, ranks, tile_owner, tile_row, tile_block):
    n = lax.axis_size("occ")
    tiles, flat = amplitudes.shape
    local_blocks, width, cols = panels.shape
    row_dev = ranks.shape[0]
    capacity = tiles // 4
    blocks = local_blocks * n
    depth = local_blocks * width
    chunks = cols // CHUNK
    others = n - 1
    chips = n // 2
    cells = row_dev * blocks
    whole = pl.BlockSpec(memory_space=pl.ANY)
    vmem = pl.BlockSpec(memory_space=pltpu.VMEM)
    dma = pltpu.SemaphoreType.DMA
    out = pl.pallas_call(
        functools.partial(kernel, n, row_dev, width, capacity),
        out_shape=pltpu.VMEM((row_dev * width, cols), jnp.bfloat16),
        in_specs=[whole] * 7,
        out_specs=vmem,
        scratch_shapes=[
            pltpu.VMEM((chunks, blocks * width, CHUNK), jnp.bfloat16),
            pltpu.VMEM((tiles, flat), jnp.bfloat16),
            pltpu.VMEM((n, 2 * capacity, flat // 2), jnp.bfloat16),
            pltpu.VMEM((n, 2 * capacity, flat // 2), jnp.bfloat16),
            pltpu.VMEM((n, 8, 128), jnp.int32),
            pltpu.VMEM((n, 8, 128), jnp.int32),
            pltpu.VMEM((flat // 128 * cells, 128), jnp.float32),
            pltpu.VMEM((blocks // 2, row_dev * width, 128), jnp.float32),
            pltpu.VMEM((row_dev * width, blocks * width), jnp.bfloat16),
            pltpu.VMEM((local_blocks, cols // width), jnp.int32),
            pltpu.VMEM((1, row_dev), jnp.int32),
            pltpu.VMEM((1, tiles), jnp.int32),
            pltpu.VMEM((1, tiles), jnp.int32),
            pltpu.VMEM((1, tiles), jnp.int32),
            dma((5,)),
            dma((chunks,)), dma,
            dma((chips - 1, chunks)), dma((chips - 1, chunks)),
            dma((chunks,)), dma((chunks,)),
            dma((chips - 1, chunks)), dma((chips - 1, chunks)),
            dma((others,)), dma((others,)), dma((others,)), dma((others,)),
        ],
        compiler_params=pltpu.CompilerParams(
            collective_id=0, has_side_effects=True, vmem_limit_bytes=VMEM_LIMIT
        ),
    )(
        panels.reshape(depth, cols), amplitudes, tile_mask, ranks[None], tile_owner[None],
        tile_row[None], tile_block[None],
    )
    return pl.pallas_call(
        write_kernel,
        out_shape=jax.ShapeDtypeStruct((row_dev * width, cols), jnp.bfloat16),
        in_specs=[vmem],
        out_specs=whole,
        scratch_shapes=[dma((PARTS,))],
        compiler_params=pltpu.CompilerParams(vmem_limit_bytes=1024 * 1024),
    )(out).reshape(row_dev, width, cols)


def solution(mesh):
    placed = (
        P(("frag", "occ"), None),
        P(("frag", "occ"), None, "vir"),
        P(("frag", "occ"), "vir"),
        P(("frag", "occ")),
        P(("frag", "occ")),
        P(("frag", "occ")),
        P(("frag", "occ")),
    )
    return jax.shard_map(
        body, mesh=mesh, in_specs=placed, out_specs=P(("frag", "occ"), None, "vir"), check_vma=False
    )
```

```python
import functools

import jax
import jax.numpy as jnp
from jax import lax
from jax.experimental import pallas as pl
from jax.experimental.pallas import tpu as pltpu
from jax.sharding import PartitionSpec as P

MESH = pl.DeviceIdType.MESH
CHUNK = 512
EARLY = 2
PARTS = 4
VMEM_LIMIT = 59 * 1024 * 1024


def kernel(
    n, row_dev, width, capacity,
    panel_hbm, amp_hbm, mask_hbm, rank_hbm, owner_hbm, row_hbm, block_hbm,
    out_ref,
    gathered, amp, outbox, inbox, code_out, code_in, cells_s, block_f32, block_bf,
    mask_ref, rank_ref, owner_ref, row_ref, block_ref, small_sem,
    load_sem, amp_sem, far_send, far_recv, mate_send, mate_recv, fwd_send, fwd_recv,
    box_send, box_recv, code_send, code_recv,
):
    me = lax.axis_index("occ")
    ranks_of_chips = n // 2
    mate = me + 1 - 2 * lax.rem(me, 2)
    chunks = gathered.shape[0]
    depth = panel_hbm.shape[0]
    local_blocks = depth // width
    blocks = local_blocks * n
    tiles = amp.shape[0]
    flat = amp.shape[1]
    half = flat // 2
    cells = row_dev * blocks

    def peer(distance):
        return lax.rem(me + distance, n)

    def slot(k, source):
        return gathered.at[k, pl.ds(pl.multiple_of(source * depth, depth), depth), :]

    def columns(k):
        return pl.ds(pl.multiple_of(k * CHUNK, CHUNK), CHUNK)

    def load(k):
        return pltpu.make_async_copy(panel_hbm.at[:, columns(k)], slot(k, me), load_sem.at[k])

    def far(k, d):
        return pltpu.make_async_remote_copy(
            src_ref=slot(k, me), dst_ref=slot(k, me),
            send_sem=far_send.at[d - 1, k], recv_sem=far_recv.at[d - 1, k],
            device_id={"occ": lax.rem(mate + 2 * d, n)}, device_id_type=MESH,
        )

    def near(k):
        return pltpu.make_async_remote_copy(
            src_ref=slot(k, me), dst_ref=slot(k, me),
            send_sem=mate_send.at[k], recv_sem=mate_recv.at[k],
            device_id={"occ": mate}, device_id_type=MESH,
        )

    def forward(k, d):
        source = lax.rem(mate + n - 2 * d, n)
        return pltpu.make_async_remote_copy(
            src_ref=slot(k, source), dst_ref=slot(k, source),
            send_sem=fwd_send.at[d - 1, k], recv_sem=fwd_recv.at[d - 1, k],
            device_id={"occ": mate}, device_id_type=MESH,
        )

    def box(d):
        target = peer(d)
        return pltpu.make_async_remote_copy(
            src_ref=outbox.at[target], dst_ref=inbox.at[me],
            send_sem=box_send.at[d - 1], recv_sem=box_recv.at[d - 1],
            device_id={"occ": target}, device_id_type=MESH,
        )

    def code(d):
        target = peer(d)
        return pltpu.make_async_remote_copy(
            src_ref=code_out.at[target], dst_ref=code_in.at[me],
            send_sem=code_send.at[d - 1], recv_sem=code_recv.at[d - 1],
            device_id={"occ": target}, device_id_type=MESH,
        )

    barrier = pltpu.get_barrier_semaphore()
    for d in range(1, n):
        pl.semaphore_signal(barrier, inc=1, device_id={"occ": peer(d)}, device_id_type=MESH)

    small = [
        pltpu.make_async_copy(source, target, small_sem.at[i])
        for i, (source, target) in enumerate((
            (mask_hbm, mask_ref), (rank_hbm, rank_ref), (owner_hbm, owner_ref),
            (row_hbm, row_ref), (block_hbm, block_ref),
        ))
    ]
    load(0).start()
    for copy in small:
        copy.start()

    @pl.loop(1, chunks)
    def _(k):
        load(k).start()

    fetch_amp = pltpu.make_async_copy(amp_hbm, amp, amp_sem)
    fetch_amp.start()

    col_tiles = mask_ref.shape[1]

    def mask_chunk(k):
        tile_of = (k * CHUNK + lax.broadcasted_iota(jnp.int32, (col_tiles, CHUNK), 1)) // width
        spread = (tile_of == lax.broadcasted_iota(jnp.int32, (col_tiles, CHUNK), 0))
        kept = jnp.dot(
            mask_ref[...].astype(jnp.float32).astype(jnp.bfloat16),
            spread.astype(jnp.float32).astype(jnp.bfloat16),
            preferred_element_type=jnp.float32,
        ).astype(jnp.bfloat16)
        load(k).wait()
        for b in range(local_blocks):
            rows = pl.ds(pl.multiple_of(me * depth + b * width, width), width)
            gathered[k, rows, :] = gathered[k, rows, :] * kept[b : b + 1, :]

    def send_chunk(k):
        for d in range(1, ranks_of_chips):
            far(k, d).start()
        near(k).start()

    early = min(EARLY, chunks)

    for copy in small:
        copy.wait()
    mask_chunk(0)
    pl.semaphore_wait(barrier, n - 1)
    send_chunk(0)

    @pl.loop(1, early)
    def _(k):
        mask_chunk(k)
        send_chunk(k)

    owner = owner_ref[...]
    tile_lane = lax.broadcasted_iota(jnp.int32, (tiles, tiles), 1)
    tile_sub = lax.broadcasted_iota(jnp.int32, (tiles, tiles), 0)
    owner_col = jnp.sum(
        jnp.where(tile_lane == tile_sub, jnp.broadcast_to(owner, (tiles, tiles)), 0),
        axis=1, keepdims=True,
    )
    same = (owner_col == owner) & (tile_sub < tile_lane)
    before = jnp.sum(same.astype(jnp.int32), axis=0, keepdims=True)
    tile_code = row_ref[...] * blocks + block_ref[...] + 1
    fetch_amp.wait()
    slot_sub = lax.rem(lax.broadcasted_iota(jnp.int32, (2 * capacity, tiles), 0), capacity)
    for o in range(n):
        chosen = (owner == o) & (before == slot_sub)
        picked = jnp.dot(
            chosen[:capacity].astype(jnp.float32).astype(jnp.bfloat16), amp[...],
            preferred_element_type=jnp.float32,
        )
        outbox[o] = jnp.concatenate([picked[:, :half], picked[:, half:]], axis=0).astype(jnp.bfloat16)
        code_col = jnp.sum(jnp.where(chosen, tile_code, 0), axis=1, keepdims=True)
        lane = lax.broadcasted_iota(jnp.int32, (2 * capacity, 128), 1)
        sub = lax.broadcasted_iota(jnp.int32, (2 * capacity, 128), 0)
        code_row = jnp.sum(jnp.where(lane == sub, code_col, 0), axis=0, keepdims=True)
        code_out[o] = jnp.broadcast_to(code_row, (8, 128))
    for d in range(1, n):
        box(d).start()
        code(d).start()

    @pl.loop(early, chunks)
    def _(k):
        mask_chunk(k)
        send_chunk(k)

    inbox[me] = outbox[me]
    code_in[me] = code_out[me]
    for d in range(1, n):
        box(d).wait()
        code(d).wait()

    cell_sub = lax.broadcasted_iota(jnp.int32, (cells, 2 * capacity), 0)
    slot_half = lax.broadcasted_iota(jnp.int32, (cells, 2 * capacity), 1) // capacity
    ranks = rank_ref[...]
    rank_lane = lax.broadcasted_iota(jnp.int32, (cells, row_dev), 1)
    cell_row = lax.broadcasted_iota(jnp.int32, (cells, row_dev), 0) // blocks
    cell_rank = jnp.sum(jnp.where(rank_lane == cell_row, ranks, 0), axis=1, keepdims=True)
    per_half = half // 128

    for h in range(2):
        total = jnp.zeros((cells, half), jnp.float32)
        for o in range(n):
            here = (code_in[o][0:1, : 2 * capacity] == cell_sub + 1) & (slot_half == h)
            total = total + jnp.dot(
                here.astype(jnp.float32).astype(jnp.bfloat16), inbox[o],
                preferred_element_type=jnp.float32,
            )
        place = h * half + lax.broadcasted_iota(jnp.int32, (cells, half), 1)
        kept = (place // width < cell_rank) & (lax.rem(place, width) < cell_rank)
        total = jnp.where(kept, total, 0.0)
        for r in range(per_half):
            start = (h * per_half + r) * cells
            cells_s[start : start + cells, :] = total[:, r * 128 : (r + 1) * 128]

    pairs = width // 2
    low = lax.broadcasted_iota(jnp.int32, (pairs, 128), 1) < width
    for row in range(row_dev):
        @pl.loop(0, blocks // 2)
        def _(q):
            first = cells_s[pl.ds(row * blocks + 2 * q, pairs, stride=cells), :]
            second = cells_s[pl.ds(row * blocks + 2 * q + 1, pairs, stride=cells), :]
            even = jnp.where(low, first, pltpu.roll(second, width, 1))
            odd = jnp.where(low, pltpu.roll(first, width, 1), second)
            block_f32[q, pl.ds(row * width, pairs, stride=2), :] = even
            block_f32[q, pl.ds(row * width + 1, pairs, stride=2), :] = odd

    for q in range(blocks // 2):
        block_bf[:, q * 128 : (q + 1) * 128] = block_f32[q].astype(jnp.bfloat16)

    def multiply(k):
        near(k).wait_recv()
        for d in range(1, ranks_of_chips):
            forward(k, d).wait_recv()
        out_ref[:, columns(k)] = jnp.dot(
            block_bf[...], gathered[k], preferred_element_type=jnp.float32
        ).astype(jnp.bfloat16)

    def pass_on(k):
        for d in range(1, ranks_of_chips):
            far(k, d).wait_recv()
            forward(k, d).start()

    pass_on(0)

    @pl.loop(1, chunks)
    def _(k):
        pass_on(k)
        multiply(k - 1)

    multiply(chunks - 1)

    @pl.loop(0, chunks)
    def _(k):
        near(k).wait_send()
        for d in range(1, ranks_of_chips):
            far(k, d).wait_send()
            forward(k, d).wait_send()


def write_kernel(held, out_hbm, out_sem):
    parts = out_sem.shape[0]
    rows = held.shape[0] // parts

    def store(k):
        place = pl.ds(k * rows, rows)
        return pltpu.make_async_copy(held.at[place, :], out_hbm.at[place, :], out_sem.at[k])

    for k in range(parts):
        store(k).start()
    for k in range(parts):
        store(k).wait()


def body(amplitudes, panels, tile_mask, ranks, tile_owner, tile_row, tile_block):
    n = lax.axis_size("occ")
    tiles, flat = amplitudes.shape
    local_blocks, width, cols = panels.shape
    row_dev = ranks.shape[0]
    capacity = tiles // 4
    blocks = local_blocks * n
    depth = local_blocks * width
    chunks = cols // CHUNK
    others = n - 1
    chips = n // 2
    cells = row_dev * blocks
    whole = pl.BlockSpec(memory_space=pl.ANY)
    vmem = pl.BlockSpec(memory_space=pltpu.VMEM)
    dma = pltpu.SemaphoreType.DMA
    out = pl.pallas_call(
        functools.partial(kernel, n, row_dev, width, capacity),
        out_shape=pltpu.VMEM((row_dev * width, cols), jnp.bfloat16),
        in_specs=[whole] * 7,
        out_specs=vmem,
        scratch_shapes=[
            pltpu.VMEM((chunks, blocks * width, CHUNK), jnp.bfloat16),
            pltpu.VMEM((tiles, flat), jnp.bfloat16),
            pltpu.VMEM((n, 2 * capacity, flat // 2), jnp.bfloat16),
            pltpu.VMEM((n, 2 * capacity, flat // 2), jnp.bfloat16),
            pltpu.VMEM((n, 8, 128), jnp.int32),
            pltpu.VMEM((n, 8, 128), jnp.int32),
            pltpu.VMEM((flat // 128 * cells, 128), jnp.float32),
            pltpu.VMEM((blocks // 2, row_dev * width, 128), jnp.float32),
            pltpu.VMEM((row_dev * width, blocks * width), jnp.bfloat16),
            pltpu.VMEM((local_blocks, cols // width), jnp.int32),
            pltpu.VMEM((1, row_dev), jnp.int32),
            pltpu.VMEM((1, tiles), jnp.int32),
            pltpu.VMEM((1, tiles), jnp.int32),
            pltpu.VMEM((1, tiles), jnp.int32),
            dma((5,)),
            dma((chunks,)), dma,
            dma((chips - 1, chunks)), dma((chips - 1, chunks)),
            dma((chunks,)), dma((chunks,)),
            dma((chips - 1, chunks)), dma((chips - 1, chunks)),
            dma((others,)), dma((others,)), dma((others,)), dma((others,)),
        ],
        compiler_params=pltpu.CompilerParams(
            collective_id=0, has_side_effects=True, vmem_limit_bytes=VMEM_LIMIT
        ),
    )(
        panels.reshape(depth, cols), amplitudes, tile_mask, ranks[None], tile_owner[None],
        tile_row[None], tile_block[None],
    )
    return pl.pallas_call(
        write_kernel,
        out_shape=jax.ShapeDtypeStruct((row_dev * width, cols), jnp.bfloat16),
        in_specs=[vmem],
        out_specs=whole,
        scratch_shapes=[dma((PARTS,))],
        compiler_params=pltpu.CompilerParams(vmem_limit_bytes=1024 * 1024),
    )(out).reshape(row_dev, width, cols)


def solution(mesh):
    placed = (
        P(("frag", "occ"), None),
        P(("frag", "occ"), None, "vir"),
        P(("frag", "occ"), "vir"),
        P(("frag", "occ")),
        P(("frag", "occ")),
        P(("frag", "occ")),
        P(("frag", "occ")),
    )
    return jax.shard_map(
        body, mesh=mesh, in_specs=placed, out_specs=P(("frag", "occ"), None, "vir"), check_vma=False
    )
```
